32 devices in a mesh: member: 16 (over z, y, x), mp: 2 (over core).
Axes of the slice: x: 2, y: 2, z: 4, core: 2. Of those that a mesh axis runs over, the one named last changes fastest.
Arguments:
- token_ids: int32 [64, 64], P('member'), may hold values from 0 to 76031
- fit_ranks: int32 [64], P('member'), may hold values from 0 to 63, as said below
- embed_table: bfloat16 [3584, 76032], P('member'), may hold values from -40 to 40
- norm_gain: float32 [3584], replicated, may hold values from 0.1 to 1.9
- qkv_weight: bfloat16 [3584, 2304], P('member', 'mp'), may hold values from -0.09375 to 0.09375
- qkv_bias: float32 [2304], P('mp'), may hold values from -3 to 3
- out_weight: bfloat16 [3584, 1792], P('member', 'mp'), may hold values from -0.125 to 0.125
- value_weight: float32 [3584], replicated, may hold values from -0.09375 to 0.09375
- qkv_left: bfloat16 [64, 3584], P('member'), may hold values from -5 to 5
- qkv_right: bfloat16 [64, 2304], P('member', 'mp'), may hold values from -5 to 5
- out_left: bfloat16 [64, 1792], P('member', 'mp'), may hold values from -5 to 5
- out_right: bfloat16 [64, 3584], P('member'), may hold values from -5 to 5
Outputs:
- values: float32 [64, 64], P(('member', 'mp'))
- qkv_grad: float32 [3584, 2304], P('member', 'mp')
- out_grad: float32 [3584, 1792], P('member', 'mp')
The draws below stay inside these ranges and needn't reach their ends.
Inputs may be any that keep to these rules, and one draw needn't show every extreme that they name: `fit_ranks`: A member's rank is the number of members whose integer fitness score is strictly lower; equal scores share a rank.
All inputs are finite; a program needn't handle non-finite values.
Results may differ from the reference program's by a relative error of at most 0.0052.
Values may be sent and summed in bfloat16 or wider, within the bound.
A program may use at most 128 MiB of HBM per device.

```python
import math
import jax
import jax.numpy as jnp
import numpy as np
from jax import lax

D = 3584
HD = 128
HQ = 14
HK = 2
V = 76032
SEQ = 64
POP = 64
BLOCKS = 2
QKV = 2304
QW = 1792


def draw_fit_ranks(key, part):
    jitter = jax.random.randint(key, (POP,), 0, 64)
    upward = jnp.arange(POP, dtype=jnp.int32) * 128 // POP
    scores = jitter + upward
    lower_count = jnp.sum((scores[None, :] < scores[:, None]).astype(jnp.int32), axis=1)
    return lower_count.astype(jnp.int32)


def draw_embed_table(key, part):
    key_rows = jax.random.fold_in(key, 11)
    key_cols = jax.random.fold_in(key, 12)
    key_body = jax.random.fold_in(key, 13)
    feature_scale = jnp.exp(jax.random.uniform(key_rows, (D, 1), jnp.float32, math.log(0.3), math.log(3.0)))
    token_scale = jnp.exp(jax.random.uniform(key_cols, (1, V), jnp.float32, math.log(0.3), math.log(3.0)))
    entries = jax.random.truncated_normal(key_body, -4.0, 4.0, (D, V), jnp.float32)
    return (entries * feature_scale * token_scale).astype(jnp.bfloat16)


def plant(values, stream_key, least, high):
    place = [jax.random.randint(jax.random.fold_in(stream_key, axis), (), 0, length) for axis, length in enumerate(values.shape)]
    widest = values.shape.index(max(values.shape))
    next_to = place[:widest] + [(place[widest] + 1) % values.shape[widest]] + place[widest + 1:]
    return values.at[tuple(place)].set(least).at[tuple(next_to)].set(high)


def level_of(stream_key, extent, cuts, low, largest):
    factor_of = 1.0
    for axis_at, parts in cuts:
        draws = jax.random.uniform(jax.random.fold_in(jax.random.fold_in(stream_key, 6), axis_at), (parts,), jnp.float32, low / len(cuts), largest / len(cuts))
        factor_of = factor_of * jnp.repeat(jnp.exp(draws), extent[axis_at] // parts).reshape((-1,) + (1,) * (len(extent) - 1 - axis_at))
    return factor_of


def wide_ids(own_key, extent, count, lean):
    loads = [min(1 << octave, count + 1 - (1 << octave)) * (1 << 20) // math.isqrt((1 << octave) ** lean) + 1 for octave in range((count + 1).bit_length()) if 1 << octave <= count]
    width = 1 + sum(loads) // (1 << 30)
    listing = np.cumsum(np.array([max(1, weight // width) for weight in loads]))
    lot = jax.random.randint(jax.random.fold_in(own_key, 1), extent, 0, int(listing[len(loads) - 1]))
    start = jnp.left_shift(1, jnp.searchsorted(jnp.asarray(listing, jnp.int32), lot, side="right").astype(jnp.int32))
    rank = start - 1 + jax.random.randint(jax.random.fold_in(own_key, 4), extent, 0, 1 << 30) % jnp.minimum(start, count + 1 - start)
    return jax.random.permutation(jax.random.fold_in(own_key, 2), count)[rank].astype(jnp.int32)


def gaussian(rng, dims, scale, limit, shards=(), kind=jnp.bfloat16):
    values = jax.random.normal(rng, dims, jnp.float32) * scale
    if len(shards) > 0:
        values = level_of(rng, dims, shards, -0.22, 0.18) * values
    return jnp.clip(values, min=-limit, max=limit).astype(kind)


def setup_inputs(seed: int = 0) -> dict:
    streams_of = jax.random.split(jax.random.key(seed), 13)
    token_ids = plant(wide_ids(streams_of[0], (POP, SEQ), V, 2), jax.random.fold_in(streams_of[0], 3), 0, V - 1).astype(jnp.int32)
    fit_ranks = draw_fit_ranks(jax.random.fold_in(streams_of[12], 71), 0)
    embed_table = draw_embed_table(jax.random.fold_in(streams_of[12], 71), 0)
    norm_gain = jnp.clip(1.0 + 0.18 * jax.random.normal(streams_of[3], (D,), jnp.float32), 0.1, 1.9)
    qkv_weight = gaussian(streams_of[4], (D, QKV), D ** -0.5, 0.09375, ((0, 16), (1, 2)))
    qkv_bias = gaussian(streams_of[5], (QKV,), 0.5, 3.0, ((0, 2),), jnp.float32)
    out_weight = gaussian(streams_of[6], (D, QW), QW ** -0.5, 0.125, ((0, 16), (1, 2)))
    value_weight = gaussian(streams_of[7], (D,), D ** -0.5, 0.09375, (), jnp.float32)
    qkv_left = gaussian(streams_of[8], (POP, D), 1.0, 5.0, ((0, 16),))
    qkv_right = gaussian(streams_of[9], (POP, QKV), 1.0, 5.0, ((0, 16), (1, 2)))
    out_left = gaussian(streams_of[10], (POP, QW), 1.0, 5.0, ((0, 16), (1, 2)))
    out_right = gaussian(streams_of[11], (POP, D), 1.0, 5.0, ((0, 16),))
    return dict(token_ids=token_ids, fit_ranks=fit_ranks, embed_table=embed_table, norm_gain=norm_gain, qkv_weight=qkv_weight, qkv_bias=qkv_bias, out_weight=out_weight, value_weight=value_weight, qkv_left=qkv_left, qkv_right=qkv_right, out_left=out_left, out_right=out_right)


SIGMA = 0.01
EPSILON = 1e-06
THETA = 1000000.0
MASKED = -1e+30

def rope_tables(length, head_size):
    halfway = head_size // 2
    inverse = THETA ** (-(jnp.arange(halfway, dtype=jnp.float32) * 2.0 / head_size))
    places = jnp.arange(length, dtype=jnp.float32)
    angles = places[:, None] * inverse[None, :]
    angles = jnp.concatenate([angles, angles], axis=1)
    return (jnp.cos(angles), jnp.sin(angles))

def rotate(states, cosine, sine_table):
    halfway = states.shape[-1] // 2
    turned = jnp.concatenate([-states[..., halfway:], states[..., :halfway]], axis=-1)
    return states * cosine[:, None, :] + turned * sine_table[:, None, :]

def reference(token_ids, fit_ranks, embed_table, norm_gain, qkv_weight, qkv_bias, out_weight, value_weight, qkv_left, qkv_right, out_left, out_right):
    group_heads = HQ // BLOCKS
    group_kv = HK // BLOCKS
    shard_width = (HQ + 2 * HK) * HD // BLOCKS
    cosine, sine_table = rope_tables(SEQ, HD)
    causal = jnp.arange(SEQ)[None, :] <= jnp.arange(SEQ)[:, None]

    def one_member(packed):
        token_row, left_in, right_in, out_in, out_back = packed
        features = jnp.take(embed_table, token_row, axis=1).T.astype(jnp.float32)
        inverse_rms = lax.rsqrt(lax.optimization_barrier(jnp.mean(features * features, axis=1, keepdims=True)) + EPSILON)
        normed = (features * inverse_rms * norm_gain[None, :]).astype(jnp.bfloat16)
        projected = jnp.dot(normed, qkv_weight, preferred_element_type=jnp.float32)
        coef_in = jnp.dot(normed, left_in, preferred_element_type=jnp.float32)
        projected = projected + SIGMA * coef_in[:, None] * right_in.astype(jnp.float32)[None, :] + qkv_bias[None, :]
        projected = projected.reshape(SEQ, BLOCKS, shard_width)
        query_heads = projected[:, :, :group_heads * HD].reshape(SEQ, HQ, HD)
        key_heads = projected[:, :, group_heads * HD:(group_heads + group_kv) * HD].reshape(SEQ, HK, HD)
        value_heads = projected[:, :, (group_heads + group_kv) * HD:].reshape(SEQ, HK, HD)
        query_heads = rotate(query_heads, cosine, sine_table).astype(jnp.bfloat16)
        key_heads = rotate(key_heads, cosine, sine_table).astype(jnp.bfloat16)
        value_heads = value_heads.astype(jnp.bfloat16)
        grouped = query_heads.reshape(SEQ, HK, HQ // HK, HD).astype(jnp.float32)
        scores = jnp.einsum('skgd,tkd->kgst', grouped, key_heads.astype(jnp.float32)) / math.sqrt(HD)
        scores = jnp.where(causal, scores, MASKED)
        top = lax.optimization_barrier(jnp.max(scores, axis=-1, keepdims=True))
        weights = jnp.exp(scores - top)
        weights = (weights / lax.optimization_barrier(jnp.sum(weights, axis=-1, keepdims=True))).astype(jnp.bfloat16)
        context = jnp.einsum('kgst,tkd->skgd', weights.astype(jnp.float32), value_heads.astype(jnp.float32))
        context = context.astype(jnp.bfloat16).reshape(SEQ, HQ * HD)
        outcome = jnp.dot(context, out_weight.T, preferred_element_type=jnp.float32)
        coef_out = jnp.dot(context, out_in, preferred_element_type=jnp.float32)
        outcome = outcome + SIGMA * coef_out[:, None] * out_back.astype(jnp.float32)[None, :]
        residual = features + outcome
        inverse_out = lax.rsqrt(lax.optimization_barrier(jnp.mean(residual * residual, axis=1, keepdims=True)) + EPSILON)
        return lax.optimization_barrier(jnp.sum(residual * inverse_out * value_weight[None, :], axis=1))
    values = lax.map(one_member, (token_ids, qkv_left, qkv_right, out_left, out_right))
    population = token_ids.shape[0]
    rank_values = fit_ranks.astype(jnp.float32)
    center = jnp.sum(rank_values) / population
    spread = jnp.sum(rank_values * rank_values) / population - center * center
    fitness = (rank_values - center) * lax.rsqrt(spread + EPSILON)
    weighted_in = qkv_left.astype(jnp.float32) * fitness[:, None]
    qkv_grad = jnp.dot(weighted_in.T, qkv_right.astype(jnp.float32), precision=lax.Precision.HIGHEST) / (population * SIGMA)
    weighted_out = out_right.astype(jnp.float32) * fitness[:, None]
    out_grad = jnp.dot(weighted_out.T, out_left.astype(jnp.float32), precision=lax.Precision.HIGHEST) / (population * SIGMA)
    return (values, qkv_grad, out_grad)
```

```python
import functools
import math

import jax
import jax.numpy as jnp
from jax import lax
from jax.experimental import pallas as pl
from jax.experimental.pallas import tpu as pltpu
from jax.sharding import PartitionSpec as P

HD = 128
HQ = 14
HK = 2


SIGMA = 0.01
EPSILON = 1e-06
THETA = 1000000.0
MASKED = -1e30


def rope_tables(length, head_size):
    halfway = head_size // 2
    inverse = THETA ** (-(jnp.arange(halfway, dtype=jnp.float32) * 2.0 / head_size))
    places = jnp.arange(length, dtype=jnp.float32)
    angles = places[:, None] * inverse[None, :]
    angles = jnp.concatenate([angles, angles], axis=1)
    return (jnp.cos(angles), jnp.sin(angles))


def rotate(states, cosine, sine_table):
    halfway = states.shape[-1] // 2
    turned = jnp.concatenate([-states[..., halfway:], states[..., :halfway]], axis=-1)
    return states * cosine[None, :, None, :] + turned * sine_table[None, :, None, :]


def attend(query_heads, key_heads, value_heads, kv_count):
    members, length, head_count, head_size = query_heads.shape
    group_size = head_count // kv_count
    grouped = query_heads.reshape(members, length, kv_count, group_size, head_size)
    scores = jnp.einsum(
        "mskgd,mtkd->mkgst", grouped, key_heads, preferred_element_type=jnp.float32
    ) / math.sqrt(head_size)
    causal = jnp.arange(length)[None, :] <= jnp.arange(length)[:, None]
    scores = jnp.where(causal, scores, MASKED)
    top = jnp.max(scores, axis=-1, keepdims=True)
    weights = jnp.exp(scores - top)
    weights = (weights / jnp.sum(weights, axis=-1, keepdims=True)).astype(jnp.bfloat16)
    context = jnp.einsum(
        "mkgst,mtkd->mskgd", weights, value_heads, preferred_element_type=jnp.float32
    )
    return context.astype(jnp.bfloat16).reshape(members, length, head_count * head_size)


def on_device(
    token_ids,
    fit_ranks,
    embed_table,
    norm_gain,
    qkv_weight,
    qkv_bias,
    out_weight,
    value_weight,
    qkv_left,
    qkv_right,
    out_left,
    out_right,
):
    members, length = token_ids.shape
    row_count = members * length
    mp_size = lax.axis_size("mp")
    heads_here = HQ // mp_size
    kv_here = HK // mp_size
    population = members * lax.axis_size("member")
    contract_rows = (((0,), (0,)), ((), ()))
    contract_cols = (((1,), (1,)), ((), ()))
    all_ids = lax.all_gather(token_ids, "member", axis=0, tiled=True)
    picked = jnp.take(embed_table, all_ids.reshape(-1), axis=1)
    embedded = lax.all_to_all(picked, "member", split_axis=1, concat_axis=0, tiled=True)
    features = embedded.astype(jnp.float32)
    inverse_rms = lax.rsqrt(jnp.mean(features * features, axis=0, keepdims=True) + EPSILON)
    normed = (features * inverse_rms * norm_gain[:, None]).astype(jnp.bfloat16)
    base_proj = lax.dot_general(
        normed,
        lax.all_gather(qkv_weight, "member", axis=0, tiled=True),
        contract_rows,
        preferred_element_type=jnp.float32,
    )
    normed_members = normed.reshape(normed.shape[0], members, length)
    coef_in = jnp.einsum("dms,md->ms", normed_members, qkv_left, preferred_element_type=jnp.float32)
    projected = (
        base_proj.reshape(members, length, -1)
        + SIGMA * coef_in[:, :, None] * qkv_right.astype(jnp.float32)[:, None, :]
        + qkv_bias[None, None, :]
    )
    query_width = heads_here * HD
    kv_width = kv_here * HD
    cosine, sine_table = rope_tables(length, HD)
    query_heads = rotate(
        projected[:, :, :query_width].reshape(members, length, heads_here, HD), cosine, sine_table
    ).astype(jnp.bfloat16)
    key_heads = rotate(
        projected[:, :, query_width : query_width + kv_width].reshape(members, length, kv_here, HD),
        cosine,
        sine_table,
    ).astype(jnp.bfloat16)
    value_heads = (
        projected[:, :, query_width + kv_width :]
        .reshape(members, length, kv_here, HD)
        .astype(jnp.bfloat16)
    )
    context = attend(query_heads, key_heads, value_heads, kv_here)
    coef_out = jnp.einsum("msq,mq->ms", context, out_left, preferred_element_type=jnp.float32)
    flat_context = context.reshape(row_count, query_width)
    share_rows = row_count // mp_size
    partial_out = lax.dot_general(
        flat_context,
        lax.all_gather(out_weight, "member", axis=0, tiled=True),
        contract_cols,
        preferred_element_type=jnp.float32,
    )
    head_term = (
        partial_out.reshape(members, length, -1)
        + SIGMA * coef_out[:, :, None] * out_right.astype(jnp.float32)[:, None, :]
    )
    summed = lax.psum_scatter(
        head_term.reshape(row_count, -1), "mp", scatter_dimension=0, tiled=True
    )
    mp_index = lax.axis_index("mp")
    own_embed = lax.dynamic_slice_in_dim(embedded, mp_index * share_rows, share_rows, 1)
    residual = own_embed.T.astype(jnp.float32) + summed
    inverse_out = lax.rsqrt(jnp.mean(residual * residual, axis=1, keepdims=True) + EPSILON)
    value_rows = jnp.sum(residual * inverse_out * value_weight[None, :], axis=1).reshape(
        members // mp_size, length
    )
    rank_values = fit_ranks.astype(jnp.float32)
    first_sum, second_sum = lax.psum(
        (jnp.sum(rank_values), jnp.sum(rank_values * rank_values)), "member"
    )
    center = first_sum / population
    spread = second_sum / population - center * center
    fit_local = (rank_values - center) * lax.rsqrt(spread + EPSILON)
    fitness = lax.all_gather(fit_local, "member", axis=0, tiled=True)
    left_rows, right_rows = (
        lax.all_to_all(qkv_left, "member", split_axis=1, concat_axis=0, tiled=True),
        lax.all_to_all(out_right, "member", split_axis=1, concat_axis=0, tiled=True),
    )
    right_cols, left_cols = (
        lax.all_gather(qkv_right, "member", axis=0, tiled=True),
        lax.all_gather(out_left, "member", axis=0, tiled=True),
    )
    weighted_in = left_rows.astype(jnp.float32) * fitness[:, None]
    qkv_grad = lax.dot_general(
        weighted_in,
        right_cols.astype(jnp.float32),
        contract_rows,
        precision=lax.Precision.HIGHEST,
        preferred_element_type=jnp.float32,
    ) / (population * SIGMA)
    weighted_out = right_rows.astype(jnp.float32) * fitness[:, None]
    out_grad = lax.dot_general(
        weighted_out,
        left_cols.astype(jnp.float32),
        contract_rows,
        precision=lax.Precision.HIGHEST,
        preferred_element_type=jnp.float32,
    ) / (population * SIGMA)
    return (value_rows, qkv_grad, out_grad)


MESH = pl.DeviceIdType.MESH
VOCAB_BLOCK = 2304
GROUP = 256
MIB = 1024 * 1024


def share_kernel(n, ids_ref, pack_ref, all_ids_ref, all_pack_ref, send_sem, recv_sem, own_sem):
    me = lax.axis_index("member")
    core = lax.axis_index("mp")
    barrier = pltpu.get_barrier_semaphore()

    def greet(k, carry):
        other = lax.rem(me + k, n)
        pl.semaphore_signal(barrier, inc=1, device_id=(other, core), device_id_type=MESH)
        return carry

    lax.fori_loop(1, n, greet, 0)
    pl.semaphore_wait(barrier, n - 1)

    def copies(k):
        other = lax.rem(me + k, n)
        return (
            pltpu.make_async_remote_copy(
                src_ref=ids_ref,
                dst_ref=all_ids_ref.at[me],
                send_sem=send_sem.at[0, k],
                recv_sem=recv_sem.at[0, k],
                device_id=(other, core),
                device_id_type=MESH,
            ),
            pltpu.make_async_remote_copy(
                src_ref=pack_ref.at[other],
                dst_ref=all_pack_ref.at[me],
                send_sem=send_sem.at[1, k],
                recv_sem=recv_sem.at[1, k],
                device_id=(other, core),
                device_id_type=MESH,
            ),
        )

    def launch(k, carry):
        for copy in copies(k):
            copy.start()
        return carry

    lax.fori_loop(1, n, launch, 0)
    own_ids = pltpu.make_async_copy(ids_ref, all_ids_ref.at[me], own_sem.at[0])
    own_pack = pltpu.make_async_copy(pack_ref.at[me], all_pack_ref.at[me], own_sem.at[1])
    own_ids.start()
    own_pack.start()
    own_ids.wait()
    own_pack.wait()

    def finish(k, carry):
        for copy in copies(k):
            copy.wait()
        return carry

    lax.fori_loop(1, n, finish, 0)


def share(ids, pack, n):
    return pl.pallas_call(
        functools.partial(share_kernel, n),
        out_shape=(
            jax.ShapeDtypeStruct((n,) + ids.shape, ids.dtype),
            jax.ShapeDtypeStruct(pack.shape, pack.dtype),
        ),
        in_specs=[pl.BlockSpec(memory_space=pltpu.VMEM)] * 2,
        out_specs=[pl.BlockSpec(memory_space=pltpu.VMEM)] * 2,
        scratch_shapes=[
            pltpu.SemaphoreType.DMA((2, n)),
            pltpu.SemaphoreType.DMA((2, n)),
            pltpu.SemaphoreType.DMA((2,)),
        ],
        compiler_params=pltpu.CompilerParams(collective_id=0, has_side_effects=True),
        name="share_small",
    )(ids, pack)


def pick_kernel(count_ref, sorted_ref, rank_ref, table_ref, out_ref, total):
    step = pl.program_id(0)
    last = pl.num_programs(0) - 1
    picks = total.shape[1]
    width = table_ref.shape[1]

    @pl.when(step == 0)
    def _():
        total[...] = jnp.zeros_like(total)

    first = count_ref[step] // GROUP
    final = (count_ref[step + 1] + GROUP - 1) // GROUP

    def group_step(g, carry):
        columns = pl.ds(pl.multiple_of(g * GROUP, GROUP), GROUP)
        local = sorted_ref[:, columns] - step * width
        entries = lax.broadcasted_iota(jnp.int32, (width, GROUP), 0)
        chosen = jnp.where(entries == local, 1.0, 0.0).astype(jnp.bfloat16)
        total[:, columns] += jnp.dot(
            table_ref[...], chosen, preferred_element_type=jnp.float32
        )
        return carry

    lax.fori_loop(first, final, group_step, 0)

    @pl.when(step == last)
    def _():
        found = total[...].astype(jnp.bfloat16)
        block = out_ref.shape[2]
        for g in range(picks // GROUP):
            ranks = rank_ref[:, g * GROUP : (g + 1) * GROUP]
            places = lax.broadcasted_iota(jnp.int32, (picks, GROUP), 0)
            moved = jnp.where(places == ranks, 1.0, 0.0).astype(jnp.bfloat16)
            back = jnp.dot(found, moved, preferred_element_type=jnp.float32).astype(jnp.bfloat16)
            for part in range(GROUP // block):
                out_ref[g * (GROUP // block) + part] = back[:, part * block : (part + 1) * block]


def pick_columns(table, ids, block):
    features, vocabulary = table.shape
    picks = ids.shape[0]
    steps = vocabulary // VOCAB_BLOCK
    keys = ids * picks + jnp.arange(picks, dtype=jnp.int32)
    ranks = jnp.sum((keys[None, :] < keys[:, None]).astype(jnp.int32), axis=1)
    places = jnp.arange(picks, dtype=jnp.int32)
    ordered = jnp.sum(jnp.where(ranks[None, :] == places[:, None], ids[None, :], 0), axis=1)
    edges = jnp.arange(steps + 1, dtype=jnp.int32) * VOCAB_BLOCK
    counts = jnp.sum((ids[None, :] < edges[:, None]).astype(jnp.int32), axis=1)
    return pl.pallas_call(
        pick_kernel,
        out_shape=jax.ShapeDtypeStruct((picks // block, features, block), jnp.bfloat16),
        grid_spec=pltpu.PrefetchScalarGridSpec(
            num_scalar_prefetch=1,
            grid=(steps,),
            in_specs=[
                pl.BlockSpec((1, picks), lambda i, c: (0, 0)),
                pl.BlockSpec((1, picks), lambda i, c: (0, 0)),
                pl.BlockSpec((features, VOCAB_BLOCK), lambda i, c: (0, i)),
            ],
            out_specs=pl.BlockSpec((picks // block, features, block), lambda i, c: (0, 0, 0)),
            scratch_shapes=[pltpu.VMEM((features, picks), jnp.float32)],
        ),
        compiler_params=pltpu.CompilerParams(
            vmem_limit_bytes=40 * MIB, dimension_semantics=("arbitrary",)
        ),
        cost_estimate=pl.CostEstimate(
            flops=2 * features * vocabulary * GROUP,
            bytes_accessed=features * vocabulary * 2,
            transcendentals=0,
        ),
        name="pick_columns",
    )(counts, ordered[None, :], ranks[None, :], table)


def deliver_kernel(n, blocks_ref, out_ref, send_sem, recv_sem, pass_send, pass_recv, own_sem):
    me = lax.axis_index("member")
    core = lax.axis_index("mp")
    features, block = blocks_ref.shape[1:]
    barrier = pltpu.get_barrier_semaphore()
    partner = (me, 1 - core)

    def greet(k, carry):
        other = lax.rem(me + k, n)
        pl.semaphore_signal(barrier, inc=1, device_id=(other, core), device_id_type=MESH)
        return carry

    lax.fori_loop(1, n, greet, 0)
    pl.semaphore_signal(barrier, inc=1, device_id=partner, device_id_type=MESH)
    pl.semaphore_wait(barrier, n)
    columns = pl.ds(pl.multiple_of(core * block, block), block)

    def place(source):
        return out_ref.at[pl.ds(pl.multiple_of(source * features, 16), features), columns]

    def across(k):
        other = lax.rem(me + k, n)
        return pltpu.make_async_remote_copy(
            src_ref=blocks_ref.at[other],
            dst_ref=place(me),
            send_sem=send_sem.at[k],
            recv_sem=recv_sem.at[k],
            device_id=(other, core),
            device_id_type=MESH,
        )

    def over(k, source_ref, source):
        return pltpu.make_async_remote_copy(
            src_ref=source_ref,
            dst_ref=place(source),
            send_sem=pass_send.at[k],
            recv_sem=pass_recv.at[k],
            device_id=partner,
            device_id_type=MESH,
        )

    def launch(k, carry):
        across(k).start()
        return carry

    lax.fori_loop(1, n, launch, 0)
    over(0, blocks_ref.at[me], me).start()
    own = pltpu.make_async_copy(blocks_ref.at[me], place(me), own_sem)
    own.start()

    def forward(k, carry):
        across(k).wait_recv()
        source = lax.rem(me + n - k, n)
        over(k, place(source), source).start()
        return carry

    lax.fori_loop(1, n, forward, 0)
    own.wait()
    over(0, blocks_ref.at[me], me).wait()

    def finish(k, carry):
        across(k).wait_send()
        source = lax.rem(me + n - k, n)
        over(k, place(source), source).wait()
        return carry

    lax.fori_loop(1, n, finish, 0)


def deliver(blocks, n):
    _, features, block = blocks.shape
    return pl.pallas_call(
        functools.partial(deliver_kernel, n),
        out_shape=jax.ShapeDtypeStruct((n * features, 2 * block), blocks.dtype),
        in_specs=[pl.BlockSpec(memory_space=pltpu.VMEM)],
        out_specs=pl.BlockSpec(memory_space=pltpu.VMEM),
        scratch_shapes=[
            pltpu.SemaphoreType.DMA((n,)),
            pltpu.SemaphoreType.DMA((n,)),
            pltpu.SemaphoreType.DMA((n,)),
            pltpu.SemaphoreType.DMA((n,)),
            pltpu.SemaphoreType.DMA,
        ],
        compiler_params=pltpu.CompilerParams(
            collective_id=1, has_side_effects=True, vmem_limit_bytes=24 * MIB
        ),
        name="deliver_embeddings",
    )(blocks)


def value_kernel(partial_ref, embed_ref, gain_ref, out_ref, landed, send_sem, recv_sem):
    me = lax.axis_index("member")
    core = lax.axis_index("mp")
    partner = (me, 1 - core)
    barrier = pltpu.get_barrier_semaphore()
    pl.semaphore_signal(barrier, inc=1, device_id=partner, device_id_type=MESH)
    pl.semaphore_wait(barrier, 1)
    share_rows = landed.shape[0]
    parts = 4
    piece = share_rows // parts

    def copy(i):
        theirs = pl.multiple_of((1 - core) * share_rows + i * piece, 8)
        return pltpu.make_async_remote_copy(
            src_ref=partial_ref.at[pl.ds(theirs, piece)],
            dst_ref=landed.at[pl.ds(i * piece, piece)],
            send_sem=send_sem.at[i],
            recv_sem=recv_sem.at[i],
            device_id=partner,
            device_id_type=MESH,
        )

    for i in range(parts):
        copy(i).start()
    for i in range(parts):
        copy(i).wait_recv()
        ours = pl.ds(pl.multiple_of(core * share_rows + i * piece, piece), piece)
        rows = (
            embed_ref[ours, :].astype(jnp.float32)
            + partial_ref[ours, :]
            + landed[i * piece : (i + 1) * piece, :]
        )
        scale = lax.rsqrt(jnp.mean(rows * rows, axis=1, keepdims=True) + EPSILON)
        out_ref[i * piece : (i + 1) * piece, :] = jnp.sum(
            rows * scale * gain_ref[...], axis=1, keepdims=True
        )
    for i in range(parts):
        copy(i).wait_send()


def value_rows_of(partial, embed, gain):
    rows, width = partial.shape
    return pl.pallas_call(
        value_kernel,
        out_shape=jax.ShapeDtypeStruct((rows // 2, 1), jnp.float32),
        in_specs=[pl.BlockSpec(memory_space=pltpu.VMEM)] * 3,
        out_specs=pl.BlockSpec(memory_space=pltpu.VMEM),
        scratch_shapes=[
            pltpu.VMEM((rows // 2, width), jnp.float32),
            pltpu.SemaphoreType.DMA((4,)),
            pltpu.SemaphoreType.DMA((4,)),
        ],
        compiler_params=pltpu.CompilerParams(
            collective_id=2, has_side_effects=True, vmem_limit_bytes=32 * MIB
        ),
        name="value_rows",
    )(partial, embed, gain[None, :])


def on_device_direct(
    token_ids,
    fit_ranks,
    embed_table,
    norm_gain,
    qkv_weight,
    qkv_bias,
    out_weight,
    value_weight,
    qkv_left,
    qkv_right,
    out_left,
    out_right,
):
    members, length = token_ids.shape
    row_count = members * length
    n = lax.axis_size("member")
    mp_size = lax.axis_size("mp")
    heads_here = HQ // mp_size
    kv_here = HK // mp_size
    population = members * n
    features = embed_table.shape[0]
    half = row_count // mp_size
    width_in = qkv_weight.shape[1]
    width_out = out_weight.shape[1]
    mp_index = lax.axis_index("mp")
    contract_rows = (((0,), (0,)), ((), ()))
    weights = lax.all_gather(
        jnp.concatenate([qkv_weight, out_weight], axis=1), "member", axis=0, tiled=True
    )
    id_rows = token_ids.reshape(mp_size, half)
    rank_row = jnp.zeros((1, half), jnp.int32).at[0, :members].set(fit_ranks)
    ids = jnp.concatenate([id_rows, rank_row, jnp.zeros((8 - mp_size - 1, half), jnp.int32)])

    def per_owner(factor):
        return factor.reshape(members, n, features).transpose(1, 0, 2).reshape(n, -1)

    common = jnp.concatenate([qkv_right.reshape(-1), out_left.reshape(-1)])
    pack = jnp.concatenate(
        [
            per_owner(qkv_left),
            per_owner(out_right),
            jnp.broadcast_to(common[None, :], (n, common.shape[0])),
        ],
        axis=1,
    )
    used = pack.shape[1]
    lines = -(-used // (16 * 128)) * 16
    pack = jnp.pad(pack, ((0, 0), (0, lines * 128 - used))).reshape(n, lines, 128)
    all_ids, all_pack = share(ids, pack, n)
    picked_ids = lax.dynamic_index_in_dim(all_ids, mp_index, 1, keepdims=False).reshape(-1)
    all_ranks = all_ids[:, mp_size, :members].reshape(-1)
    embedded = deliver(pick_columns(embed_table, picked_ids, half), n)

    rows = embedded.T
    states = rows.astype(jnp.float32)
    inverse_rms = lax.rsqrt(jnp.mean(states * states, axis=1, keepdims=True) + EPSILON)
    normed = (states * inverse_rms * norm_gain[None, :]).astype(jnp.bfloat16)
    base_proj = jnp.dot(normed, weights[:, :width_in], preferred_element_type=jnp.float32)
    coef_in = jnp.einsum(
        "msd,md->ms",
        normed.reshape(members, length, -1),
        qkv_left,
        preferred_element_type=jnp.float32,
    )
    projected = (
        base_proj.reshape(members, length, -1)
        + SIGMA * coef_in[:, :, None] * qkv_right.astype(jnp.float32)[:, None, :]
        + qkv_bias[None, None, :]
    )
    query_width = heads_here * HD
    kv_width = kv_here * HD
    cosine, sine_table = rope_tables(length, HD)
    query_heads = rotate(
        projected[:, :, :query_width].reshape(members, length, heads_here, HD), cosine, sine_table
    ).astype(jnp.bfloat16)
    key_heads = rotate(
        projected[:, :, query_width : query_width + kv_width].reshape(members, length, kv_here, HD),
        cosine,
        sine_table,
    ).astype(jnp.bfloat16)
    value_heads = (
        projected[:, :, query_width + kv_width :]
        .reshape(members, length, kv_here, HD)
        .astype(jnp.bfloat16)
    )
    context = attend(query_heads, key_heads, value_heads, kv_here)
    coef_out = jnp.einsum("msq,mq->ms", context, out_left, preferred_element_type=jnp.float32)
    partial_out = lax.dot_general(
        context.reshape(row_count, query_width),
        weights[:, width_in:],
        (((1,), (1,)), ((), ())),
        preferred_element_type=jnp.float32,
    )
    head_term = (
        partial_out.reshape(members, length, -1)
        + SIGMA * coef_out[:, :, None] * out_right.astype(jnp.float32)[:, None, :]
    )
    value_rows = value_rows_of(head_term.reshape(row_count, -1), rows, value_weight).reshape(
        members // mp_size, length
    )

    rank_values = all_ranks.astype(jnp.float32)
    center = jnp.sum(rank_values) / population
    spread = jnp.sum(rank_values * rank_values) / population - center * center
    fitness = (rank_values - center) * lax.rsqrt(spread + EPSILON)
    flat = all_pack.reshape(n, -1)
    edge = 0
    factors = []
    for width in (features, features, width_in, width_out):
        piece = flat[:, edge : edge + members * width]
        factors.append(piece.reshape(population, width).astype(jnp.float32))
        edge += members * width
    left_rows, right_rows, right_cols, left_cols = factors
    grads = [
        lax.dot_general(
            mine * fitness[:, None],
            theirs,
            contract_rows,
            precision=lax.Precision.HIGHEST,
            preferred_element_type=jnp.float32,
        )
        / (population * SIGMA)
        for mine, theirs in ((left_rows, right_cols), (right_rows, left_cols))
    ]
    return (value_rows, grads[0], grads[1])


def fits_direct(mesh):
    return mesh.shape["mp"] == 2 and mesh.shape["member"] == 16


def solution(mesh):
    placed = (
        P("member", None),
        P("member"),
        P("member", None),
        P(),
        P("member", "mp"),
        P("mp"),
        P("member", "mp"),
        P(),
        P("member", None),
        P("member", "mp"),
        P("member", "mp"),
        P("member", None),
    )
    return jax.shard_map(
        on_device_direct if fits_direct(mesh) else on_device,
        mesh=mesh,
        in_specs=placed,
        out_specs=(P(("member", "mp"), None), P("member", "mp"), P("member", "mp")),
        check_vma=False,
    )
```

```python
import functools
import math

import jax
import jax.numpy as jnp
from jax import lax
from jax.experimental import pallas as pl
from jax.experimental.pallas import tpu as pltpu
from jax.sharding import PartitionSpec as P

HD = 128
HQ = 14
HK = 2


SIGMA = 0.01
EPSILON = 1e-06
THETA = 1000000.0
MASKED = -1e30


def rope_tables(length, head_size):
    halfway = head_size // 2
    inverse = THETA ** (-(jnp.arange(halfway, dtype=jnp.float32) * 2.0 / head_size))
    places = jnp.arange(length, dtype=jnp.float32)
    angles = places[:, None] * inverse[None, :]
    angles = jnp.concatenate([angles, angles], axis=1)
    return (jnp.cos(angles), jnp.sin(angles))


def rotate(states, cosine, sine_table):
    halfway = states.shape[-1] // 2
    turned = jnp.concatenate([-states[..., halfway:], states[..., :halfway]], axis=-1)
    return states * cosine[None, :, None, :] + turned * sine_table[None, :, None, :]


def attend(query_heads, key_heads, value_heads, kv_count):
    members, length, head_count, head_size = query_heads.shape
    group_size = head_count // kv_count
    grouped = query_heads.reshape(members, length, kv_count, group_size, head_size)
    scores = jnp.einsum(
        "mskgd,mtkd->mkgst", grouped, key_heads, preferred_element_type=jnp.float32
    ) / math.sqrt(head_size)
    causal = jnp.arange(length)[None, :] <= jnp.arange(length)[:, None]
    scores = jnp.where(causal, scores, MASKED)
    top = jnp.max(scores, axis=-1, keepdims=True)
    weights = jnp.exp(scores - top)
    weights = (weights / jnp.sum(weights, axis=-1, keepdims=True)).astype(jnp.bfloat16)
    context = jnp.einsum(
        "mkgst,mtkd->mskgd", weights, value_heads, preferred_element_type=jnp.float32
    )
    return context.astype(jnp.bfloat16).reshape(members, length, head_count * head_size)


def on_device(
    token_ids,
    fit_ranks,
    embed_table,
    norm_gain,
    qkv_weight,
    qkv_bias,
    out_weight,
    value_weight,
    qkv_left,
    qkv_right,
    out_left,
    out_right,
):
    members, length = token_ids.shape
    row_count = members * length
    mp_size = lax.axis_size("mp")
    heads_here = HQ // mp_size
    kv_here = HK // mp_size
    population = members * lax.axis_size("member")
    contract_rows = (((0,), (0,)), ((), ()))
    contract_cols = (((1,), (1,)), ((), ()))
    all_ids = lax.all_gather(token_ids, "member", axis=0, tiled=True)
    picked = jnp.take(embed_table, all_ids.reshape(-1), axis=1)
    embedded = lax.all_to_all(picked, "member", split_axis=1, concat_axis=0, tiled=True)
    features = embedded.astype(jnp.float32)
    inverse_rms = lax.rsqrt(jnp.mean(features * features, axis=0, keepdims=True) + EPSILON)
    normed = (features * inverse_rms * norm_gain[:, None]).astype(jnp.bfloat16)
    base_proj = lax.dot_general(
        normed,
        lax.all_gather(qkv_weight, "member", axis=0, tiled=True),
        contract_rows,
        preferred_element_type=jnp.float32,
    )
    normed_members = normed.reshape(normed.shape[0], members, length)
    coef_in = jnp.einsum("dms,md->ms", normed_members, qkv_left, preferred_element_type=jnp.float32)
    projected = (
        base_proj.reshape(members, length, -1)
        + SIGMA * coef_in[:, :, None] * qkv_right.astype(jnp.float32)[:, None, :]
        + qkv_bias[None, None, :]
    )
    query_width = heads_here * HD
    kv_width = kv_here * HD
    cosine, sine_table = rope_tables(length, HD)
    query_heads = rotate(
        projected[:, :, :query_width].reshape(members, length, heads_here, HD), cosine, sine_table
    ).astype(jnp.bfloat16)
    key_heads = rotate(
        projected[:, :, query_width : query_width + kv_width].reshape(members, length, kv_here, HD),
        cosine,
        sine_table,
    ).astype(jnp.bfloat16)
    value_heads = (
        projected[:, :, query_width + kv_width :]
        .reshape(members, length, kv_here, HD)
        .astype(jnp.bfloat16)
    )
    context = attend(query_heads, key_heads, value_heads, kv_here)
    coef_out = jnp.einsum("msq,mq->ms", context, out_left, preferred_element_type=jnp.float32)
    flat_context = context.reshape(row_count, query_width)
    share_rows = row_count // mp_size
    partial_out = lax.dot_general(
        flat_context,
        lax.all_gather(out_weight, "member", axis=0, tiled=True),
        contract_cols,
        preferred_element_type=jnp.float32,
    )
    head_term = (
        partial_out.reshape(members, length, -1)
        + SIGMA * coef_out[:, :, None] * out_right.astype(jnp.float32)[:, None, :]
    )
    summed = lax.psum_scatter(
        head_term.reshape(row_count, -1), "mp", scatter_dimension=0, tiled=True
    )
    mp_index = lax.axis_index("mp")
    own_embed = lax.dynamic_slice_in_dim(embedded, mp_index * share_rows, share_rows, 1)
    residual = own_embed.T.astype(jnp.float32) + summed
    inverse_out = lax.rsqrt(jnp.mean(residual * residual, axis=1, keepdims=True) + EPSILON)
    value_rows = jnp.sum(residual * inverse_out * value_weight[None, :], axis=1).reshape(
        members // mp_size, length
    )
    rank_values = fit_ranks.astype(jnp.float32)
    first_sum, second_sum = lax.psum(
        (jnp.sum(rank_values), jnp.sum(rank_values * rank_values)), "member"
    )
    center = first_sum / population
    spread = second_sum / population - center * center
    fit_local = (rank_values - center) * lax.rsqrt(spread + EPSILON)
    fitness = lax.all_gather(fit_local, "member", axis=0, tiled=True)
    left_rows, right_rows = (
        lax.all_to_all(qkv_left, "member", split_axis=1, concat_axis=0, tiled=True),
        lax.all_to_all(out_right, "member", split_axis=1, concat_axis=0, tiled=True),
    )
    right_cols, left_cols = (
        lax.all_gather(qkv_right, "member", axis=0, tiled=True),
        lax.all_gather(out_left, "member", axis=0, tiled=True),
    )
    weighted_in = left_rows.astype(jnp.float32) * fitness[:, None]
    qkv_grad = lax.dot_general(
        weighted_in,
        right_cols.astype(jnp.float32),
        contract_rows,
        precision=lax.Precision.HIGHEST,
        preferred_element_type=jnp.float32,
    ) / (population * SIGMA)
    weighted_out = right_rows.astype(jnp.float32) * fitness[:, None]
    out_grad = lax.dot_general(
        weighted_out,
        left_cols.astype(jnp.float32),
        contract_rows,
        precision=lax.Precision.HIGHEST,
        preferred_element_type=jnp.float32,
    ) / (population * SIGMA)
    return (value_rows, qkv_grad, out_grad)


MESH = pl.DeviceIdType.MESH
VOCAB_BLOCK = 2304
GROUP = 256
PLANE = 4
RELAYED = 5 * HD
MIB = 1024 * 1024


def share_kernel(n, ids_ref, pack_ref, all_ids_ref, all_pack_ref, send_sem, recv_sem, own_sem):
    me = lax.axis_index("member")
    core = lax.axis_index("mp")
    barrier = pltpu.get_barrier_semaphore()

    def greet(k, carry):
        other = lax.rem(me + k, n)
        pl.semaphore_signal(barrier, inc=1, device_id=(other, core), device_id_type=MESH)
        return carry

    lax.fori_loop(1, n, greet, 0)
    pl.semaphore_wait(barrier, n - 1)

    def copies(k):
        other = lax.rem(me + k, n)
        return (
            pltpu.make_async_remote_copy(
                src_ref=ids_ref,
                dst_ref=all_ids_ref.at[me],
                send_sem=send_sem.at[0, k],
                recv_sem=recv_sem.at[0, k],
                device_id=(other, core),
                device_id_type=MESH,
            ),
            pltpu.make_async_remote_copy(
                src_ref=pack_ref.at[other],
                dst_ref=all_pack_ref.at[me],
                send_sem=send_sem.at[1, k],
                recv_sem=recv_sem.at[1, k],
                device_id=(other, core),
                device_id_type=MESH,
            ),
        )

    def launch(k, carry):
        for copy in copies(k):
            copy.start()
        return carry

    lax.fori_loop(1, n, launch, 0)
    own_ids = pltpu.make_async_copy(ids_ref, all_ids_ref.at[me], own_sem.at[0])
    own_pack = pltpu.make_async_copy(pack_ref.at[me], all_pack_ref.at[me], own_sem.at[1])
    own_ids.start()
    own_pack.start()
    own_ids.wait()
    own_pack.wait()

    def finish(k, carry):
        for copy in copies(k):
            copy.wait()
        return carry

    lax.fori_loop(1, n, finish, 0)


def share(ids, pack, n):
    return pl.pallas_call(
        functools.partial(share_kernel, n),
        out_shape=(
            jax.ShapeDtypeStruct((n,) + ids.shape, ids.dtype),
            jax.ShapeDtypeStruct(pack.shape, pack.dtype),
        ),
        in_specs=[pl.BlockSpec(memory_space=pltpu.VMEM)] * 2,
        out_specs=[pl.BlockSpec(memory_space=pltpu.VMEM)] * 2,
        scratch_shapes=[
            pltpu.SemaphoreType.DMA((2, n)),
            pltpu.SemaphoreType.DMA((2, n)),
            pltpu.SemaphoreType.DMA((2,)),
        ],
        compiler_params=pltpu.CompilerParams(collective_id=0, has_side_effects=True),
        name="share_small",
    )(ids, pack)


def pick_kernel(count_ref, sorted_ref, rank_ref, table_ref, out_ref, total):
    step = pl.program_id(0)
    last = pl.num_programs(0) - 1
    picks = total.shape[1]
    width = table_ref.shape[1]

    @pl.when(step == 0)
    def _():
        total[...] = jnp.zeros_like(total)

    first = count_ref[step] // GROUP
    final = (count_ref[step + 1] + GROUP - 1) // GROUP

    def group_step(g, carry):
        columns = pl.ds(pl.multiple_of(g * GROUP, GROUP), GROUP)
        local = sorted_ref[:, columns] - step * width
        entries = lax.broadcasted_iota(jnp.int32, (width, GROUP), 0)
        chosen = jnp.where(entries == local, 1.0, 0.0).astype(jnp.bfloat16)
        total[:, columns] += jnp.dot(
            table_ref[...], chosen, preferred_element_type=jnp.float32
        )
        return carry

    lax.fori_loop(first, final, group_step, 0)

    @pl.when(step == last)
    def _():
        found = total[...].astype(jnp.bfloat16)
        block = out_ref.shape[2]
        for g in range(picks // GROUP):
            ranks = rank_ref[:, g * GROUP : (g + 1) * GROUP]
            places = lax.broadcasted_iota(jnp.int32, (picks, GROUP), 0)
            moved = jnp.where(places == ranks, 1.0, 0.0).astype(jnp.bfloat16)
            back = jnp.dot(found, moved, preferred_element_type=jnp.float32).astype(jnp.bfloat16)
            for part in range(GROUP // block):
                out_ref[g * (GROUP // block) + part] = back[:, part * block : (part + 1) * block]


def pick_columns(table, ids, block):
    features, vocabulary = table.shape
    picks = ids.shape[0]
    steps = vocabulary // VOCAB_BLOCK
    keys = ids * picks + jnp.arange(picks, dtype=jnp.int32)
    ranks = jnp.sum((keys[None, :] < keys[:, None]).astype(jnp.int32), axis=1)
    places = jnp.arange(picks, dtype=jnp.int32)
    ordered = jnp.sum(jnp.where(ranks[None, :] == places[:, None], ids[None, :], 0), axis=1)
    edges = jnp.arange(steps + 1, dtype=jnp.int32) * VOCAB_BLOCK
    counts = jnp.sum((ids[None, :] < edges[:, None]).astype(jnp.int32), axis=1)
    return pl.pallas_call(
        pick_kernel,
        out_shape=jax.ShapeDtypeStruct((picks // block, features, block), jnp.bfloat16),
        grid_spec=pltpu.PrefetchScalarGridSpec(
            num_scalar_prefetch=1,
            grid=(steps,),
            in_specs=[
                pl.BlockSpec((1, picks), lambda i, c: (0, 0)),
                pl.BlockSpec((1, picks), lambda i, c: (0, 0)),
                pl.BlockSpec((features, VOCAB_BLOCK), lambda i, c: (0, i)),
            ],
            out_specs=pl.BlockSpec((picks // block, features, block), lambda i, c: (0, 0, 0)),
            scratch_shapes=[pltpu.VMEM((features, picks), jnp.float32)],
        ),
        compiler_params=pltpu.CompilerParams(
            vmem_limit_bytes=40 * MIB, dimension_semantics=("arbitrary",)
        ),
        cost_estimate=pl.CostEstimate(
            flops=2 * features * vocabulary * GROUP,
            bytes_accessed=features * vocabulary * 2,
            transcendentals=0,
        ),
        name="pick_columns",
    )(counts, ordered[None, :], ranks[None, :], table)


def deliver_kernel(
    n,
    blocks_ref,
    weight_ref,
    out_ref,
    all_ref,
    send_sem,
    recv_sem,
    pass_send,
    pass_recv,
    own_sem,
    line_send,
    line_recv,
    side_send,
    side_recv,
    far_send,
    far_recv,
):
    me = lax.axis_index("member")
    core = lax.axis_index("mp")
    features, block = blocks_ref.shape[1:]
    barrier = pltpu.get_barrier_semaphore()
    partner = (me, 1 - core)

    def greet(k, carry):
        other = lax.rem(me + k, n)
        pl.semaphore_signal(barrier, inc=1, device_id=(other, core), device_id_type=MESH)
        return carry

    lax.fori_loop(1, n, greet, 0)
    pl.semaphore_signal(barrier, inc=1, device_id=partner, device_id_type=MESH)
    pl.semaphore_wait(barrier, n)
    columns = pl.ds(pl.multiple_of(core * block, block), block)

    def place(source):
        return out_ref.at[pl.ds(pl.multiple_of(source * features, 16), features), columns]

    def across(k):
        other = lax.rem(me + k, n)
        return pltpu.make_async_remote_copy(
            src_ref=blocks_ref.at[other],
            dst_ref=place(me),
            send_sem=send_sem.at[k],
            recv_sem=recv_sem.at[k],
            device_id=(other, core),
            device_id_type=MESH,
        )

    def over(k, source_ref, source):
        return pltpu.make_async_remote_copy(
            src_ref=source_ref,
            dst_ref=place(source),
            send_sem=pass_send.at[k],
            recv_sem=pass_recv.at[k],
            device_id=partner,
            device_id_type=MESH,
        )

    layer = me // PLANE
    spot = lax.rem(me, PLANE)
    depth = n // PLANE
    half_rows = weight_ref.shape[0] // 2
    flips = (lax.rem(spot, 2), spot // 2)
    beside = (spot + 1 - 2 * flips[0], spot + 2 - 4 * flips[1])

    def owner(k, where):
        return lax.rem(layer + depth - k, depth) * PLANE + where

    def along(k):
        other = lax.rem(layer + k, depth) * PLANE + spot
        return pltpu.make_async_remote_copy(
            src_ref=weight_ref,
            dst_ref=all_ref.at[me],
            send_sem=line_send.at[k],
            recv_sem=line_recv.at[k],
            device_id=(other, core),
            device_id_type=MESH,
        )

    def aside(side, k):
        source = owner(k, spot)
        return pltpu.make_async_remote_copy(
            src_ref=weight_ref if k == 0 else all_ref.at[source],
            dst_ref=all_ref.at[source],
            send_sem=side_send.at[side, k],
            recv_sem=side_recv.at[side, k],
            device_id=(layer * PLANE + beside[side], core),
            device_id_type=MESH,
        )

    def onward(side, k):
        piece = all_ref.at[owner(k, beside[side]), pl.ds(side * half_rows, half_rows)]
        return pltpu.make_async_remote_copy(
            src_ref=piece,
            dst_ref=piece,
            send_sem=far_send.at[side, k],
            recv_sem=far_recv.at[side, k],
            device_id=(layer * PLANE + beside[1 - side], core),
            device_id_type=MESH,
        )

    for k in range(1, depth):
        along(k).start()

    def launch(k, carry):
        across(k).start()
        return carry

    lax.fori_loop(1, n, launch, 0)
    over(0, blocks_ref.at[me], me).start()
    own = pltpu.make_async_copy(blocks_ref.at[me], place(me), own_sem.at[0])
    own.start()
    own_weight = pltpu.make_async_copy(weight_ref, all_ref.at[me], own_sem.at[1])
    own_weight.start()
    for side in range(2):
        aside(side, 0).start()
    for k in range(1, depth):
        along(k).wait_recv()
        for side in range(2):
            aside(side, k).start()

    def forward(k, carry):
        across(k).wait_recv()
        source = lax.rem(me + n - k, n)
        over(k, place(source), source).start()
        return carry

    lax.fori_loop(1, n, forward, 0)
    for k in range(depth):
        for side in range(2):
            aside(side, k).wait_recv()
            onward(side, k).start()
    own.wait()
    own_weight.wait()
    over(0, blocks_ref.at[me], me).wait()

    def finish(k, carry):
        across(k).wait_send()
        source = lax.rem(me + n - k, n)
        over(k, place(source), source).wait()
        return carry

    lax.fori_loop(1, n, finish, 0)
    for k in range(1, depth):
        along(k).wait_send()
    for k in range(depth):
        for side in range(2):
            aside(side, k).wait_send()
            onward(side, k).wait()


def deliver(blocks, weight, n):
    _, features, block = blocks.shape
    return pl.pallas_call(
        functools.partial(deliver_kernel, n),
        out_shape=(
            jax.ShapeDtypeStruct((n * features, 2 * block), blocks.dtype),
            jax.ShapeDtypeStruct((n,) + weight.shape, weight.dtype),
        ),
        in_specs=[pl.BlockSpec(memory_space=pltpu.VMEM), pl.BlockSpec(memory_space=pl.ANY)],
        out_specs=[pl.BlockSpec(memory_space=pltpu.VMEM), pl.BlockSpec(memory_space=pl.ANY)],
        scratch_shapes=[
            pltpu.SemaphoreType.DMA((n,)),
            pltpu.SemaphoreType.DMA((n,)),
            pltpu.SemaphoreType.DMA((n,)),
            pltpu.SemaphoreType.DMA((n,)),
            pltpu.SemaphoreType.DMA((2,)),
            pltpu.SemaphoreType.DMA((n // PLANE,)),
            pltpu.SemaphoreType.DMA((n // PLANE,)),
            pltpu.SemaphoreType.DMA((2, n // PLANE)),
            pltpu.SemaphoreType.DMA((2, n // PLANE)),
            pltpu.SemaphoreType.DMA((2, n // PLANE)),
            pltpu.SemaphoreType.DMA((2, n // PLANE)),
        ],
        compiler_params=pltpu.CompilerParams(
            collective_id=1, has_side_effects=True, vmem_limit_bytes=24 * MIB
        ),
        name="deliver_embeddings",
    )(blocks, weight)


def value_kernel(partial_ref, embed_ref, gain_ref, out_ref, landed, send_sem, recv_sem):
    me = lax.axis_index("member")
    core = lax.axis_index("mp")
    partner = (me, 1 - core)
    barrier = pltpu.get_barrier_semaphore()
    pl.semaphore_signal(barrier, inc=1, device_id=partner, device_id_type=MESH)
    pl.semaphore_wait(barrier, 1)
    share_rows = landed.shape[0]
    parts = 4
    piece = share_rows // parts

    def copy(i):
        theirs = pl.multiple_of((1 - core) * share_rows + i * piece, 8)
        return pltpu.make_async_remote_copy(
            src_ref=partial_ref.at[pl.ds(theirs, piece)],
            dst_ref=landed.at[pl.ds(i * piece, piece)],
            send_sem=send_sem.at[i],
            recv_sem=recv_sem.at[i],
            device_id=partner,
            device_id_type=MESH,
        )

    for i in range(parts):
        copy(i).start()
    for i in range(parts):
        copy(i).wait_recv()
        ours = pl.ds(pl.multiple_of(core * share_rows + i * piece, piece), piece)
        rows = (
            embed_ref[ours, :].astype(jnp.float32)
            + partial_ref[ours, :]
            + landed[i * piece : (i + 1) * piece, :]
        )
        scale = lax.rsqrt(jnp.mean(rows * rows, axis=1, keepdims=True) + EPSILON)
        out_ref[i * piece : (i + 1) * piece, :] = jnp.sum(
            rows * scale * gain_ref[...], axis=1, keepdims=True
        )
    for i in range(parts):
        copy(i).wait_send()


def value_rows_of(partial, embed, gain):
    rows, width = partial.shape
    return pl.pallas_call(
        value_kernel,
        out_shape=jax.ShapeDtypeStruct((rows // 2, 1), jnp.float32),
        in_specs=[pl.BlockSpec(memory_space=pltpu.VMEM)] * 3,
        out_specs=pl.BlockSpec(memory_space=pltpu.VMEM),
        scratch_shapes=[
            pltpu.VMEM((rows // 2, width), jnp.float32),
            pltpu.SemaphoreType.DMA((4,)),
            pltpu.SemaphoreType.DMA((4,)),
        ],
        compiler_params=pltpu.CompilerParams(
            collective_id=2, has_side_effects=True, vmem_limit_bytes=32 * MIB
        ),
        name="value_rows",
    )(partial, embed, gain[None, :])


def on_device_direct(
    token_ids,
    fit_ranks,
    embed_table,
    norm_gain,
    qkv_weight,
    qkv_bias,
    out_weight,
    value_weight,
    qkv_left,
    qkv_right,
    out_left,
    out_right,
):
    members, length = token_ids.shape
    row_count = members * length
    n = lax.axis_size("member")
    mp_size = lax.axis_size("mp")
    heads_here = HQ // mp_size
    kv_here = HK // mp_size
    population = members * n
    features = embed_table.shape[0]
    half = row_count // mp_size
    width_in = qkv_weight.shape[1]
    width_out = out_weight.shape[1]
    mp_index = lax.axis_index("mp")
    contract_rows = (((0,), (0,)), ((), ()))
    kept = width_out - RELAYED
    weights = lax.all_gather(
        jnp.concatenate([qkv_weight, out_weight[:, :kept]], axis=1), "member", axis=0, tiled=True
    )
    id_rows = token_ids.reshape(mp_size, half)
    rank_row = jnp.zeros((1, half), jnp.int32).at[0, :members].set(fit_ranks)
    ids = jnp.concatenate([id_rows, rank_row, jnp.zeros((8 - mp_size - 1, half), jnp.int32)])

    def per_owner(factor):
        return factor.reshape(members, n, features).transpose(1, 0, 2).reshape(n, -1)

    common = jnp.concatenate([qkv_right.reshape(-1), out_left.reshape(-1)])
    pack = jnp.concatenate(
        [
            per_owner(qkv_left),
            per_owner(out_right),
            jnp.broadcast_to(common[None, :], (n, common.shape[0])),
        ],
        axis=1,
    )
    used = pack.shape[1]
    lines = -(-used // (16 * 128)) * 16
    pack = jnp.pad(pack, ((0, 0), (0, lines * 128 - used))).reshape(n, lines, 128)
    all_ids, all_pack = share(ids, pack, n)
    picked_ids = lax.dynamic_index_in_dim(all_ids, mp_index, 1, keepdims=False).reshape(-1)
    all_ranks = all_ids[:, mp_size, :members].reshape(-1)
    embedded, relayed = deliver(
        pick_columns(embed_table, picked_ids, half), out_weight[:, kept:], n
    )

    rows = embedded.T
    states = rows.astype(jnp.float32)
    inverse_rms = lax.rsqrt(jnp.mean(states * states, axis=1, keepdims=True) + EPSILON)
    normed = (states * inverse_rms * norm_gain[None, :]).astype(jnp.bfloat16)
    base_proj = jnp.dot(normed, weights[:, :width_in], preferred_element_type=jnp.float32)
    coef_in = jnp.einsum(
        "msd,md->ms",
        normed.reshape(members, length, -1),
        qkv_left,
        preferred_element_type=jnp.float32,
    )
    projected = (
        base_proj.reshape(members, length, -1)
        + SIGMA * coef_in[:, :, None] * qkv_right.astype(jnp.float32)[:, None, :]
        + qkv_bias[None, None, :]
    )
    query_width = heads_here * HD
    kv_width = kv_here * HD
    cosine, sine_table = rope_tables(length, HD)
    query_heads = rotate(
        projected[:, :, :query_width].reshape(members, length, heads_here, HD), cosine, sine_table
    ).astype(jnp.bfloat16)
    key_heads = rotate(
        projected[:, :, query_width : query_width + kv_width].reshape(members, length, kv_here, HD),
        cosine,
        sine_table,
    ).astype(jnp.bfloat16)
    value_heads = (
        projected[:, :, query_width + kv_width :]
        .reshape(members, length, kv_here, HD)
        .astype(jnp.bfloat16)
    )
    context = attend(query_heads, key_heads, value_heads, kv_here)
    coef_out = jnp.einsum("msq,mq->ms", context, out_left, preferred_element_type=jnp.float32)
    flat_context = context.reshape(row_count, query_width)
    contract_cols = (((1,), (1,)), ((), ()))
    partial_out = lax.dot_general(
        flat_context[:, :kept],
        weights[:, width_in:],
        contract_cols,
        preferred_element_type=jnp.float32,
    ) + lax.dot_general(
        flat_context[:, kept:],
        relayed.reshape(n * features, -1),
        contract_cols,
        preferred_element_type=jnp.float32,
    )
    head_term = (
        partial_out.reshape(members, length, -1)
        + SIGMA * coef_out[:, :, None] * out_right.astype(jnp.float32)[:, None, :]
    )
    value_rows = value_rows_of(head_term.reshape(row_count, -1), rows, value_weight).reshape(
        members // mp_size, length
    )

    rank_values = all_ranks.astype(jnp.float32)
    center = jnp.sum(rank_values) / population
    spread = jnp.sum(rank_values * rank_values) / population - center * center
    fitness = (rank_values - center) * lax.rsqrt(spread + EPSILON)
    flat = all_pack.reshape(n, -1)
    edge = 0
    factors = []
    for width in (features, features, width_in, width_out):
        piece = flat[:, edge : edge + members * width]
        factors.append(piece.reshape(population, width).astype(jnp.float32))
        edge += members * width
    left_rows, right_rows, right_cols, left_cols = factors
    grads = [
        lax.dot_general(
            mine * fitness[:, None],
            theirs,
            contract_rows,
            precision=lax.Precision.HIGHEST,
            preferred_element_type=jnp.float32,
        )
        / (population * SIGMA)
        for mine, theirs in ((left_rows, right_cols), (right_rows, left_cols))
    ]
    return (value_rows, grads[0], grads[1])


def fits_direct(mesh):
    return mesh.shape["mp"] == 2 and mesh.shape["member"] == 16


def solution(mesh):
    placed = (
        P("member", None),
        P("member"),
        P("member", None),
        P(),
        P("member", "mp"),
        P("mp"),
        P("member", "mp"),
        P(),
        P("member", None),
        P("member", "mp"),
        P("member", "mp"),
        P("member", None),
    )
    return jax.shard_map(
        on_device_direct if fits_direct(mesh) else on_device,
        mesh=mesh,
        in_specs=placed,
        out_specs=(P(("member", "mp"), None), P("member", "mp"), P("member", "mp")),
        check_vma=False,
    )
```

```python
import functools
import math

import jax
import jax.numpy as jnp
from jax import lax
from jax.experimental import pallas as pl
from jax.experimental.pallas import tpu as pltpu
from jax.sharding import PartitionSpec as P

HD = 128
HQ = 14
HK = 2


SIGMA = 0.01
EPSILON = 1e-06
THETA = 1000000.0
MASKED = -1e30


def rope_tables(length, head_size):
    halfway = head_size // 2
    inverse = THETA ** (-(jnp.arange(halfway, dtype=jnp.float32) * 2.0 / head_size))
    places = jnp.arange(length, dtype=jnp.float32)
    angles = places[:, None] * inverse[None, :]
    angles = jnp.concatenate([angles, angles], axis=1)
    return (jnp.cos(angles), jnp.sin(angles))


def rotate(states, cosine, sine_table):
    halfway = states.shape[-1] // 2
    turned = jnp.concatenate([-states[..., halfway:], states[..., :halfway]], axis=-1)
    return states * cosine[None, :, None, :] + turned * sine_table[None, :, None, :]


def attend(query_heads, key_heads, value_heads, kv_count):
    members, length, head_count, head_size = query_heads.shape
    group_size = head_count // kv_count
    grouped = query_heads.reshape(members, length, kv_count, group_size, head_size)
    scores = jnp.einsum(
        "mskgd,mtkd->mkgst", grouped, key_heads, preferred_element_type=jnp.float32
    ) / math.sqrt(head_size)
    causal = jnp.arange(length)[None, :] <= jnp.arange(length)[:, None]
    scores = jnp.where(causal, scores, MASKED)
    top = jnp.max(scores, axis=-1, keepdims=True)
    weights = jnp.exp(scores - top)
    weights = (weights / jnp.sum(weights, axis=-1, keepdims=True)).astype(jnp.bfloat16)
    context = jnp.einsum(
        "mkgst,mtkd->mskgd", weights, value_heads, preferred_element_type=jnp.float32
    )
    return context.astype(jnp.bfloat16).reshape(members, length, head_count * head_size)


def on_device(
    token_ids,
    fit_ranks,
    embed_table,
    norm_gain,
    qkv_weight,
    qkv_bias,
    out_weight,
    value_weight,
    qkv_left,
    qkv_right,
    out_left,
    out_right,
):
    members, length = token_ids.shape
    row_count = members * length
    mp_size = lax.axis_size("mp")
    heads_here = HQ // mp_size
    kv_here = HK // mp_size
    population = members * lax.axis_size("member")
    contract_rows = (((0,), (0,)), ((), ()))
    contract_cols = (((1,), (1,)), ((), ()))
    all_ids = lax.all_gather(token_ids, "member", axis=0, tiled=True)
    picked = jnp.take(embed_table, all_ids.reshape(-1), axis=1)
    embedded = lax.all_to_all(picked, "member", split_axis=1, concat_axis=0, tiled=True)
    features = embedded.astype(jnp.float32)
    inverse_rms = lax.rsqrt(jnp.mean(features * features, axis=0, keepdims=True) + EPSILON)
    normed = (features * inverse_rms * norm_gain[:, None]).astype(jnp.bfloat16)
    base_proj = lax.dot_general(
        normed,
        lax.all_gather(qkv_weight, "member", axis=0, tiled=True),
        contract_rows,
        preferred_element_type=jnp.float32,
    )
    normed_members = normed.reshape(normed.shape[0], members, length)
    coef_in = jnp.einsum("dms,md->ms", normed_members, qkv_left, preferred_element_type=jnp.float32)
    projected = (
        base_proj.reshape(members, length, -1)
        + SIGMA * coef_in[:, :, None] * qkv_right.astype(jnp.float32)[:, None, :]
        + qkv_bias[None, None, :]
    )
    query_width = heads_here * HD
    kv_width = kv_here * HD
    cosine, sine_table = rope_tables(length, HD)
    query_heads = rotate(
        projected[:, :, :query_width].reshape(members, length, heads_here, HD), cosine, sine_table
    ).astype(jnp.bfloat16)
    key_heads = rotate(
        projected[:, :, query_width : query_width + kv_width].reshape(members, length, kv_here, HD),
        cosine,
        sine_table,
    ).astype(jnp.bfloat16)
    value_heads = (
        projected[:, :, query_width + kv_width :]
        .reshape(members, length, kv_here, HD)
        .astype(jnp.bfloat16)
    )
    context = attend(query_heads, key_heads, value_heads, kv_here)
    coef_out = jnp.einsum("msq,mq->ms", context, out_left, preferred_element_type=jnp.float32)
    flat_context = context.reshape(row_count, query_width)
    share_rows = row_count // mp_size
    partial_out = lax.dot_general(
        flat_context,
        lax.all_gather(out_weight, "member", axis=0, tiled=True),
        contract_cols,
        preferred_element_type=jnp.float32,
    )
    head_term = (
        partial_out.reshape(members, length, -1)
        + SIGMA * coef_out[:, :, None] * out_right.astype(jnp.float32)[:, None, :]
    )
    summed = lax.psum_scatter(
        head_term.reshape(row_count, -1), "mp", scatter_dimension=0, tiled=True
    )
    mp_index = lax.axis_index("mp")
    own_embed = lax.dynamic_slice_in_dim(embedded, mp_index * share_rows, share_rows, 1)
    residual = own_embed.T.astype(jnp.float32) + summed
    inverse_out = lax.rsqrt(jnp.mean(residual * residual, axis=1, keepdims=True) + EPSILON)
    value_rows = jnp.sum(residual * inverse_out * value_weight[None, :], axis=1).reshape(
        members // mp_size, length
    )
    rank_values = fit_ranks.astype(jnp.float32)
    first_sum, second_sum = lax.psum(
        (jnp.sum(rank_values), jnp.sum(rank_values * rank_values)), "member"
    )
    center = first_sum / population
    spread = second_sum / population - center * center
    fit_local = (rank_values - center) * lax.rsqrt(spread + EPSILON)
    fitness = lax.all_gather(fit_local, "member", axis=0, tiled=True)
    left_rows, right_rows = (
        lax.all_to_all(qkv_left, "member", split_axis=1, concat_axis=0, tiled=True),
        lax.all_to_all(out_right, "member", split_axis=1, concat_axis=0, tiled=True),
    )
    right_cols, left_cols = (
        lax.all_gather(qkv_right, "member", axis=0, tiled=True),
        lax.all_gather(out_left, "member", axis=0, tiled=True),
    )
    weighted_in = left_rows.astype(jnp.float32) * fitness[:, None]
    qkv_grad = lax.dot_general(
        weighted_in,
        right_cols.astype(jnp.float32),
        contract_rows,
        precision=lax.Precision.HIGHEST,
        preferred_element_type=jnp.float32,
    ) / (population * SIGMA)
    weighted_out = right_rows.astype(jnp.float32) * fitness[:, None]
    out_grad = lax.dot_general(
        weighted_out,
        left_cols.astype(jnp.float32),
        contract_rows,
        precision=lax.Precision.HIGHEST,
        preferred_element_type=jnp.float32,
    ) / (population * SIGMA)
    return (value_rows, qkv_grad, out_grad)


MESH = pl.DeviceIdType.MESH
VOCAB_BLOCK = 2304
GROUP = 256
PLANE = 4
RELAYED = 3 * HD
MIB = 1024 * 1024


def share_kernel(n, ids_ref, pack_ref, all_ids_ref, all_pack_ref, send_sem, recv_sem, own_sem):
    me = lax.axis_index("member")
    core = lax.axis_index("mp")
    barrier = pltpu.get_barrier_semaphore()

    def greet(k, carry):
        other = lax.rem(me + k, n)
        pl.semaphore_signal(barrier, inc=1, device_id=(other, core), device_id_type=MESH)
        return carry

    lax.fori_loop(1, n, greet, 0)
    pl.semaphore_wait(barrier, n - 1)

    def copies(k):
        other = lax.rem(me + k, n)
        return (
            pltpu.make_async_remote_copy(
                src_ref=ids_ref,
                dst_ref=all_ids_ref.at[me],
                send_sem=send_sem.at[0, k],
                recv_sem=recv_sem.at[0, k],
                device_id=(other, core),
                device_id_type=MESH,
            ),
            pltpu.make_async_remote_copy(
                src_ref=pack_ref.at[other],
                dst_ref=all_pack_ref.at[me],
                send_sem=send_sem.at[1, k],
                recv_sem=recv_sem.at[1, k],
                device_id=(other, core),
                device_id_type=MESH,
            ),
        )

    def launch(k, carry):
        for copy in copies(k):
            copy.start()
        return carry

    lax.fori_loop(1, n, launch, 0)
    own_ids = pltpu.make_async_copy(ids_ref, all_ids_ref.at[me], own_sem.at[0])
    own_pack = pltpu.make_async_copy(pack_ref.at[me], all_pack_ref.at[me], own_sem.at[1])
    own_ids.start()
    own_pack.start()
    own_ids.wait()
    own_pack.wait()

    def finish(k, carry):
        for copy in copies(k):
            copy.wait()
        return carry

    lax.fori_loop(1, n, finish, 0)


def share(ids, pack, n):
    return pl.pallas_call(
        functools.partial(share_kernel, n),
        out_shape=(
            jax.ShapeDtypeStruct((n,) + ids.shape, ids.dtype),
            jax.ShapeDtypeStruct(pack.shape, pack.dtype),
        ),
        in_specs=[pl.BlockSpec(memory_space=pltpu.VMEM)] * 2,
        out_specs=[pl.BlockSpec(memory_space=pltpu.VMEM)] * 2,
        scratch_shapes=[
            pltpu.SemaphoreType.DMA((2, n)),
            pltpu.SemaphoreType.DMA((2, n)),
            pltpu.SemaphoreType.DMA((2,)),
        ],
        compiler_params=pltpu.CompilerParams(collective_id=0, has_side_effects=True),
        name="share_small",
    )(ids, pack)


def pick_kernel(count_ref, sorted_ref, rank_ref, table_ref, out_ref, total):
    step = pl.program_id(0)
    last = pl.num_programs(0) - 1
    picks = total.shape[1]
    width = table_ref.shape[1]

    @pl.when(step == 0)
    def _():
        total[...] = jnp.zeros_like(total)

    first = count_ref[step] // GROUP
    final = (count_ref[step + 1] + GROUP - 1) // GROUP

    def group_step(g, carry):
        columns = pl.ds(pl.multiple_of(g * GROUP, GROUP), GROUP)
        local = sorted_ref[:, columns] - step * width
        entries = lax.broadcasted_iota(jnp.int32, (width, GROUP), 0)
        chosen = jnp.where(entries == local, 1.0, 0.0).astype(jnp.bfloat16)
        total[:, columns] += jnp.dot(
            table_ref[...], chosen, preferred_element_type=jnp.float32
        )
        return carry

    lax.fori_loop(first, final, group_step, 0)

    @pl.when(step == last)
    def _():
        found = total[...].astype(jnp.bfloat16)
        block = out_ref.shape[2]
        for g in range(picks // GROUP):
            ranks = rank_ref[:, g * GROUP : (g + 1) * GROUP]
            places = lax.broadcasted_iota(jnp.int32, (picks, GROUP), 0)
            moved = jnp.where(places == ranks, 1.0, 0.0).astype(jnp.bfloat16)
            back = jnp.dot(found, moved, preferred_element_type=jnp.float32).astype(jnp.bfloat16)
            for part in range(GROUP // block):
                out_ref[g * (GROUP // block) + part] = back[:, part * block : (part + 1) * block]


def pick_columns(table, ids, block):
    features, vocabulary = table.shape
    picks = ids.shape[0]
    steps = vocabulary // VOCAB_BLOCK
    keys = ids * picks + jnp.arange(picks, dtype=jnp.int32)
    ranks = jnp.sum((keys[None, :] < keys[:, None]).astype(jnp.int32), axis=1)
    places = jnp.arange(picks, dtype=jnp.int32)
    ordered = jnp.sum(jnp.where(ranks[None, :] == places[:, None], ids[None, :], 0), axis=1)
    edges = jnp.arange(steps + 1, dtype=jnp.int32) * VOCAB_BLOCK
    counts = jnp.sum((ids[None, :] < edges[:, None]).astype(jnp.int32), axis=1)
    return pl.pallas_call(
        pick_kernel,
        out_shape=jax.ShapeDtypeStruct((picks // block, features, block), jnp.bfloat16),
        grid_spec=pltpu.PrefetchScalarGridSpec(
            num_scalar_prefetch=1,
            grid=(steps,),
            in_specs=[
                pl.BlockSpec((1, picks), lambda i, c: (0, 0)),
                pl.BlockSpec((1, picks), lambda i, c: (0, 0)),
                pl.BlockSpec((features, VOCAB_BLOCK), lambda i, c: (0, i)),
            ],
            out_specs=pl.BlockSpec((picks // block, features, block), lambda i, c: (0, 0, 0)),
            scratch_shapes=[pltpu.VMEM((features, picks), jnp.float32)],
        ),
        compiler_params=pltpu.CompilerParams(
            vmem_limit_bytes=40 * MIB, dimension_semantics=("arbitrary",)
        ),
        cost_estimate=pl.CostEstimate(
            flops=2 * features * vocabulary * GROUP,
            bytes_accessed=features * vocabulary * 2,
            transcendentals=0,
        ),
        name="pick_columns",
    )(counts, ordered[None, :], ranks[None, :], table)


def deliver_kernel(
    n,
    blocks_ref,
    weight_ref,
    out_ref,
    all_ref,
    send_sem,
    recv_sem,
    pass_send,
    pass_recv,
    own_sem,
    line_send,
    line_recv,
    side_send,
    side_recv,
    far_send,
    far_recv,
):
    me = lax.axis_index("member")
    core = lax.axis_index("mp")
    features, block = blocks_ref.shape[1:]
    barrier = pltpu.get_barrier_semaphore()
    partner = (me, 1 - core)

    def greet(k, carry):
        other = lax.rem(me + k, n)
        pl.semaphore_signal(barrier, inc=1, device_id=(other, core), device_id_type=MESH)
        return carry

    lax.fori_loop(1, n, greet, 0)
    pl.semaphore_signal(barrier, inc=1, device_id=partner, device_id_type=MESH)
    pl.semaphore_wait(barrier, n)
    columns = pl.ds(pl.multiple_of(core * block, block), block)

    def place(source):
        return out_ref.at[pl.ds(pl.multiple_of(source * features, 16), features), columns]

    def across(k):
        other = lax.rem(me + k, n)
        return pltpu.make_async_remote_copy(
            src_ref=blocks_ref.at[other],
            dst_ref=place(me),
            send_sem=send_sem.at[k],
            recv_sem=recv_sem.at[k],
            device_id=(other, core),
            device_id_type=MESH,
        )

    def over(k, source_ref, source):
        return pltpu.make_async_remote_copy(
            src_ref=source_ref,
            dst_ref=place(source),
            send_sem=pass_send.at[k],
            recv_sem=pass_recv.at[k],
            device_id=partner,
            device_id_type=MESH,
        )

    layer = me // PLANE
    spot = lax.rem(me, PLANE)
    depth = n // PLANE
    half_rows = weight_ref.shape[0] // 2
    flips = (lax.rem(spot, 2), spot // 2)
    beside = (spot + 1 - 2 * flips[0], spot + 2 - 4 * flips[1])

    def owner(k, where):
        return lax.rem(layer + depth - k, depth) * PLANE + where

    def along(k):
        other = lax.rem(layer + k, depth) * PLANE + spot
        return pltpu.make_async_remote_copy(
            src_ref=weight_ref,
            dst_ref=all_ref.at[me],
            send_sem=line_send.at[k],
            recv_sem=line_recv.at[k],
            device_id=(other, core),
            device_id_type=MESH,
        )

    def aside(side, k):
        source = owner(k, spot)
        return pltpu.make_async_remote_copy(
            src_ref=weight_ref if k == 0 else all_ref.at[source],
            dst_ref=all_ref.at[source],
            send_sem=side_send.at[side, k],
            recv_sem=side_recv.at[side, k],
            device_id=(layer * PLANE + beside[side], core),
            device_id_type=MESH,
        )

    def onward(side, k):
        piece = all_ref.at[owner(k, beside[side]), pl.ds(side * half_rows, half_rows)]
        return pltpu.make_async_remote_copy(
            src_ref=piece,
            dst_ref=piece,
            send_sem=far_send.at[side, k],
            recv_sem=far_recv.at[side, k],
            device_id=(layer * PLANE + beside[1 - side], core),
            device_id_type=MESH,
        )

    for k in range(1, depth):
        along(k).start()

    def launch(k, carry):
        across(k).start()
        return carry

    lax.fori_loop(1, n, launch, 0)
    over(0, blocks_ref.at[me], me).start()
    own = pltpu.make_async_copy(blocks_ref.at[me], place(me), own_sem.at[0])
    own.start()
    own_weight = pltpu.make_async_copy(weight_ref, all_ref.at[me], own_sem.at[1])
    own_weight.start()
    for side in range(2):
        aside(side, 0).start()
    for k in range(1, depth):
        along(k).wait_recv()
        for side in range(2):
            aside(side, k).start()

    def forward(k, carry):
        across(k).wait_recv()
        source = lax.rem(me + n - k, n)
        over(k, place(source), source).start()
        return carry

    lax.fori_loop(1, n, forward, 0)
    for k in range(depth):
        for side in range(2):
            aside(side, k).wait_recv()
            onward(side, k).start()
    own.wait()
    own_weight.wait()
    over(0, blocks_ref.at[me], me).wait()

    def finish(k, carry):
        across(k).wait_send()
        source = lax.rem(me + n - k, n)
        over(k, place(source), source).wait()
        return carry

    lax.fori_loop(1, n, finish, 0)
    for k in range(1, depth):
        along(k).wait_send()
    for k in range(depth):
        for side in range(2):
            aside(side, k).wait_send()
            onward(side, k).wait()


def deliver(blocks, weight, n):
    _, features, block = blocks.shape
    return pl.pallas_call(
        functools.partial(deliver_kernel, n),
        out_shape=(
            jax.ShapeDtypeStruct((n * features, 2 * block), blocks.dtype),
            jax.ShapeDtypeStruct((n,) + weight.shape, weight.dtype),
        ),
        in_specs=[pl.BlockSpec(memory_space=pltpu.VMEM), pl.BlockSpec(memory_space=pl.ANY)],
        out_specs=[pl.BlockSpec(memory_space=pltpu.VMEM), pl.BlockSpec(memory_space=pl.ANY)],
        scratch_shapes=[
            pltpu.SemaphoreType.DMA((n,)),
            pltpu.SemaphoreType.DMA((n,)),
            pltpu.SemaphoreType.DMA((n,)),
            pltpu.SemaphoreType.DMA((n,)),
            pltpu.SemaphoreType.DMA((2,)),
            pltpu.SemaphoreType.DMA((n // PLANE,)),
            pltpu.SemaphoreType.DMA((n // PLANE,)),
            pltpu.SemaphoreType.DMA((2, n // PLANE)),
            pltpu.SemaphoreType.DMA((2, n // PLANE)),
            pltpu.SemaphoreType.DMA((2, n // PLANE)),
            pltpu.SemaphoreType.DMA((2, n // PLANE)),
        ],
        compiler_params=pltpu.CompilerParams(
            collective_id=1, has_side_effects=True, vmem_limit_bytes=24 * MIB
        ),
        name="deliver_embeddings",
    )(blocks, weight)


def value_kernel(partial_ref, embed_ref, gain_ref, out_ref, landed, send_sem, recv_sem):
    me = lax.axis_index("member")
    core = lax.axis_index("mp")
    partner = (me, 1 - core)
    barrier = pltpu.get_barrier_semaphore()
    pl.semaphore_signal(barrier, inc=1, device_id=partner, device_id_type=MESH)
    pl.semaphore_wait(barrier, 1)
    share_rows = landed.shape[0]
    parts = 4
    piece = share_rows // parts

    def copy(i):
        theirs = pl.multiple_of((1 - core) * share_rows + i * piece, 8)
        return pltpu.make_async_remote_copy(
            src_ref=partial_ref.at[pl.ds(theirs, piece)],
            dst_ref=landed.at[pl.ds(i * piece, piece)],
            send_sem=send_sem.at[i],
            recv_sem=recv_sem.at[i],
            device_id=partner,
            device_id_type=MESH,
        )

    for i in range(parts):
        copy(i).start()
    for i in range(parts):
        copy(i).wait_recv()
        ours = pl.ds(pl.multiple_of(core * share_rows + i * piece, piece), piece)
        rows = (
            embed_ref[ours, :].astype(jnp.float32)
            + partial_ref[ours, :]
            + landed[i * piece : (i + 1) * piece, :]
        )
        scale = lax.rsqrt(jnp.mean(rows * rows, axis=1, keepdims=True) + EPSILON)
        out_ref[i * piece : (i + 1) * piece, :] = jnp.sum(
            rows * scale * gain_ref[...], axis=1, keepdims=True
        )
    for i in range(parts):
        copy(i).wait_send()


def value_rows_of(partial, embed, gain):
    rows, width = partial.shape
    return pl.pallas_call(
        value_kernel,
        out_shape=jax.ShapeDtypeStruct((rows // 2, 1), jnp.float32),
        in_specs=[pl.BlockSpec(memory_space=pltpu.VMEM)] * 3,
        out_specs=pl.BlockSpec(memory_space=pltpu.VMEM),
        scratch_shapes=[
            pltpu.VMEM((rows // 2, width), jnp.float32),
            pltpu.SemaphoreType.DMA((4,)),
            pltpu.SemaphoreType.DMA((4,)),
        ],
        compiler_params=pltpu.CompilerParams(
            collective_id=2, has_side_effects=True, vmem_limit_bytes=32 * MIB
        ),
        name="value_rows",
    )(partial, embed, gain[None, :])


def on_device_direct(
    token_ids,
    fit_ranks,
    embed_table,
    norm_gain,
    qkv_weight,
    qkv_bias,
    out_weight,
    value_weight,
    qkv_left,
    qkv_right,
    out_left,
    out_right,
):
    members, length = token_ids.shape
    row_count = members * length
    n = lax.axis_size("member")
    mp_size = lax.axis_size("mp")
    heads_here = HQ // mp_size
    kv_here = HK // mp_size
    population = members * n
    features = embed_table.shape[0]
    half = row_count // mp_size
    width_in = qkv_weight.shape[1]
    width_out = out_weight.shape[1]
    mp_index = lax.axis_index("mp")
    contract_rows = (((0,), (0,)), ((), ()))
    kept = width_out - RELAYED
    weights = lax.all_gather(
        jnp.concatenate([qkv_weight, out_weight[:, :kept]], axis=1), "member", axis=0, tiled=True
    )
    id_rows = token_ids.reshape(mp_size, half)
    rank_row = jnp.zeros((1, half), jnp.int32).at[0, :members].set(fit_ranks)
    ids = jnp.concatenate([id_rows, rank_row, jnp.zeros((8 - mp_size - 1, half), jnp.int32)])

    def per_owner(factor):
        return factor.reshape(members, n, features).transpose(1, 0, 2).reshape(n, -1)

    common = jnp.concatenate([qkv_right.reshape(-1), out_left.reshape(-1)])
    pack = jnp.concatenate(
        [
            per_owner(qkv_left),
            per_owner(out_right),
            jnp.broadcast_to(common[None, :], (n, common.shape[0])),
        ],
        axis=1,
    )
    used = pack.shape[1]
    lines = -(-used // (16 * 128)) * 16
    pack = jnp.pad(pack, ((0, 0), (0, lines * 128 - used))).reshape(n, lines, 128)
    all_ids, all_pack = share(ids, pack, n)
    picked_ids = lax.dynamic_index_in_dim(all_ids, mp_index, 1, keepdims=False).reshape(-1)
    all_ranks = all_ids[:, mp_size, :members].reshape(-1)
    embedded, relayed = deliver(
        pick_columns(embed_table, picked_ids, half), out_weight[:, kept:], n
    )

    rows = embedded.T
    states = rows.astype(jnp.float32)
    inverse_rms = lax.rsqrt(jnp.mean(states * states, axis=1, keepdims=True) + EPSILON)
    normed = (states * inverse_rms * norm_gain[None, :]).astype(jnp.bfloat16)
    base_proj = jnp.dot(normed, weights[:, :width_in], preferred_element_type=jnp.float32)
    coef_in = jnp.einsum(
        "msd,md->ms",
        normed.reshape(members, length, -1),
        qkv_left,
        preferred_element_type=jnp.float32,
    )
    projected = (
        base_proj.reshape(members, length, -1)
        + SIGMA * coef_in[:, :, None] * qkv_right.astype(jnp.float32)[:, None, :]
        + qkv_bias[None, None, :]
    )
    query_width = heads_here * HD
    kv_width = kv_here * HD
    cosine, sine_table = rope_tables(length, HD)
    query_heads = rotate(
        projected[:, :, :query_width].reshape(members, length, heads_here, HD), cosine, sine_table
    ).astype(jnp.bfloat16)
    key_heads = rotate(
        projected[:, :, query_width : query_width + kv_width].reshape(members, length, kv_here, HD),
        cosine,
        sine_table,
    ).astype(jnp.bfloat16)
    value_heads = (
        projected[:, :, query_width + kv_width :]
        .reshape(members, length, kv_here, HD)
        .astype(jnp.bfloat16)
    )
    context = attend(query_heads, key_heads, value_heads, kv_here)
    coef_out = jnp.einsum("msq,mq->ms", context, out_left, preferred_element_type=jnp.float32)
    flat_context = context.reshape(row_count, query_width)
    contract_cols = (((1,), (1,)), ((), ()))
    partial_out = lax.dot_general(
        flat_context[:, :kept],
        weights[:, width_in:],
        contract_cols,
        preferred_element_type=jnp.float32,
    ) + lax.dot_general(
        flat_context[:, kept:],
        relayed.reshape(n * features, -1),
        contract_cols,
        preferred_element_type=jnp.float32,
    )
    head_term = (
        partial_out.reshape(members, length, -1)
        + SIGMA * coef_out[:, :, None] * out_right.astype(jnp.float32)[:, None, :]
    )
    value_rows = value_rows_of(head_term.reshape(row_count, -1), rows, value_weight).reshape(
        members // mp_size, length
    )

    rank_values = all_ranks.astype(jnp.float32)
    center = jnp.sum(rank_values) / population
    spread = jnp.sum(rank_values * rank_values) / population - center * center
    fitness = (rank_values - center) * lax.rsqrt(spread + EPSILON)
    flat = all_pack.reshape(n, -1)
    edge = 0
    factors = []
    for width in (features, features, width_in, width_out):
        piece = flat[:, edge : edge + members * width]
        factors.append(piece.reshape(population, width).astype(jnp.float32))
        edge += members * width
    left_rows, right_rows, right_cols, left_cols = factors
    grads = [
        lax.dot_general(
            mine * fitness[:, None],
            theirs,
            contract_rows,
            precision=lax.Precision.HIGHEST,
            preferred_element_type=jnp.float32,
        )
        / (population * SIGMA)
        for mine, theirs in ((left_rows, right_cols), (right_rows, left_cols))
    ]
    return (value_rows, grads[0], grads[1])


def fits_direct(mesh):
    return mesh.shape["mp"] == 2 and mesh.shape["member"] == 16


def solution(mesh):
    placed = (
        P("member", None),
        P("member"),
        P("member", None),
        P(),
        P("member", "mp"),
        P("mp"),
        P("member", "mp"),
        P(),
        P("member", None),
        P("member", "mp"),
        P("member", "mp"),
        P("member", None),
    )
    return jax.shard_map(
        on_device_direct if fits_direct(mesh) else on_device,
        mesh=mesh,
        in_specs=placed,
        out_specs=(P(("member", "mp"), None), P("member", "mp"), P("member", "mp")),
        check_vma=False,
    )
```
